128 devices in a mesh: ctx: 16 (over z, x_lo, core), tp: 4 (over y), dp: 2 (over x_hi).
Axes of the slice: x: 4 (x_hi: 2, x_lo: 2; x = x_hi * 2 + x_lo), y: 4, z: 4, core: 2. Of those that a mesh axis runs over, the one named last changes fastest.
Arguments:
- queries: bfloat16 [16384, 2048], P(('dp', 'ctx'), 'tp'), parts along dimension 0, may hold values from -6 to 6
- keys: bfloat16 [16384, 512], P(('dp', 'ctx'), 'tp'), parts along dimension 0, may hold values from -6 to 6
- values: bfloat16 [16384, 512], P(('dp', 'ctx'), 'tp'), parts along dimension 0, may hold values from -6 to 6
- outputs: bfloat16 [16384, 2048], P(('dp', 'ctx'), 'tp'), parts along dimension 0, may hold values from -4 to 4
- out_grads: bfloat16 [16384, 2048], P(('dp', 'ctx'), 'tp'), parts along dimension 0, may hold values from -6 to 6
- log_norms: float32 [16, 16384], P('tp', ('dp', 'ctx')), parts along dimension 1, may hold values from 3 to 6
- stretch_order: int32 [64], P('dp'), parts along dimension 0, may hold values from 0 to 31, each once
Outputs:
- grad_queries: bfloat16 [16384, 2048], P(('dp', 'ctx'), 'tp'), parts along dimension 0
- grad_keys: bfloat16 [16384, 512], P(('dp', 'ctx'), 'tp'), parts along dimension 0
- grad_values: bfloat16 [16384, 512], P(('dp', 'ctx'), 'tp'), parts along dimension 0
The draws below stay inside these ranges and needn't reach their ends.
There are 2 independent parts, one for each index of `dp`. The reference program is written for one: setup_inputs(seed, part) draws one part's arguments, and reference() takes and returns one part's arrays. A program takes and returns all parts, laid end to end along the dimension named above; each array names one. Nothing has to cross between parts.
Inputs may be any that keep to these rules, and one draw needn't show every extreme that they name: stretch_order is a permutation of the 32 sequence blocks of 256 tokens.
All inputs are finite; a program needn't handle non-finite values.
Results may differ from the reference program's by a relative error of at most 0.023.
Values may be sent and summed in bfloat16 or wider, within the bound.
A program may use at most 64 MiB of HBM per device.

```python
import jax
import jax.numpy as jnp
from jax import lax

QH = 16
KVH = 4
HD = 128
STRETCH = 256
SEQ = 8192
N_CTX = 16


def block_levels(stream_key, extent, shards, low, top_value):
    def one(axis_at, shards_of):
        draws = jax.random.uniform(jax.random.fold_in(jax.random.fold_in(stream_key, 6), axis_at), (shards_of,), jnp.float32, low / len(shards), top_value / len(shards))
        return jnp.repeat(jnp.exp(draws), extent[axis_at] // shards_of).reshape((-1,) + (1,) * (len(extent) - axis_at - 1))

    factor_of = one(*shards[0])
    for cut in shards[1:]:
        factor_of = factor_of * one(*cut)
    return factor_of


def centred(stream_key, extent, spread, reach, shards=(), kind=jnp.bfloat16):
    drawn = spread * jax.random.normal(stream_key, extent, jnp.float32)
    if shards:
        drawn = drawn * block_levels(stream_key, extent, shards, -0.22, 0.18)
    return jnp.clip(drawn, -reach, reach).astype(kind)


def setup_inputs(seed: int = 0, part: int = 0) -> dict:
    key_of = jax.random.split(jax.random.key(seed), 8)
    part_keys = jax.random.split(jax.random.fold_in(key_of[7], part), 8)
    return {
        "queries": centred(part_keys[0], (SEQ, QH * HD), 1.0, 6.0, ((0, 16), (1, 4))),
        "keys": centred(part_keys[1], (SEQ, KVH * HD), 1.0, 6.0, ((0, 16), (1, 4))),
        "values": centred(part_keys[2], (SEQ, KVH * HD), 1.0, 6.0, ((0, 16), (1, 4))),
        "outputs": centred(part_keys[3], (SEQ, QH * HD), 0.3, 4.0, ((0, 16), (1, 4))),
        "out_grads": centred(part_keys[4], (SEQ, QH * HD), 1.0, 6.0, ((0, 16), (1, 4))),
        "log_norms": jnp.clip(3.0 + 3.0 * jax.random.uniform(part_keys[5], (QH, SEQ), jnp.float32) ** block_levels(part_keys[5], (QH, SEQ), ((0, 4), (1, 16)), -0.2, 0.2), 3.0, 6.0),
        "stretch_order": jax.random.permutation(part_keys[6], 2 * N_CTX).astype(jnp.int32),
    }


def reference(queries, keys, values, outputs, out_grads, log_norms, stretch_order):
    seq_len = queries.shape[0]
    group_size = QH // KVH
    score_scale = HD ** -0.5
    row_index = jnp.arange(seq_len, dtype=jnp.int32)
    position = jnp.take(stretch_order, row_index // STRETCH) * STRETCH + row_index % STRETCH
    allowed = position[None, :] <= position[:, None]
    query_heads = queries.reshape(seq_len, KVH, group_size, HD).transpose(1, 2, 0, 3)
    grad_heads = out_grads.reshape(seq_len, KVH, group_size, HD).transpose(1, 2, 0, 3)
    output_heads = outputs.reshape(seq_len, KVH, group_size, HD).transpose(1, 2, 0, 3)
    key_heads = keys.reshape(seq_len, KVH, HD).transpose(1, 0, 2)
    value_heads = values.reshape(seq_len, KVH, HD).transpose(1, 0, 2)
    norm_heads = log_norms.reshape(KVH, group_size, seq_len)

    def one_head(operands):
        query_one, grad_one, output_one, key_one, value_one, norm_one = operands
        query_f = query_one.astype(jnp.float32)
        grad_f = grad_one.astype(jnp.float32)
        key_f = key_one.astype(jnp.float32)
        value_f = value_one.astype(jnp.float32)
        delta_rows = jnp.sum(grad_f * output_one.astype(jnp.float32), axis=-1)
        scores = jnp.einsum("gqd,kd->gqk", query_f, key_f) * score_scale
        probs = jnp.where(allowed[None], jnp.exp(scores - norm_one[:, :, None]), jnp.float32(0.0))
        probs_low = probs.astype(jnp.bfloat16).astype(jnp.float32)
        grad_value = jnp.einsum("gqk,gqd->kd", probs_low, grad_f)
        grad_probs = jnp.einsum("gqd,kd->gqk", grad_f, value_f)
        grad_scores = (score_scale * probs * (grad_probs - delta_rows[:, :, None])).astype(jnp.bfloat16).astype(jnp.float32)
        grad_query = jnp.einsum("gqk,kd->gqd", grad_scores, key_f)
        grad_key = jnp.einsum("gqk,gqd->kd", grad_scores, query_f)
        return grad_query, grad_key, grad_value

    grad_query, grad_key, grad_value = lax.map(one_head, (query_heads, grad_heads, output_heads, key_heads, value_heads, norm_heads))
    grad_queries = grad_query.transpose(2, 0, 1, 3).reshape(seq_len, QH * HD).astype(jnp.bfloat16)
    grad_keys = grad_key.transpose(1, 0, 2).reshape(seq_len, KVH * HD).astype(jnp.bfloat16)
    grad_values = grad_value.transpose(1, 0, 2).reshape(seq_len, KVH * HD).astype(jnp.bfloat16)
    return (grad_queries, grad_keys, grad_values)
```

```python
import functools

import jax
import jax.numpy as jnp
from jax import lax
from jax.experimental import pallas as pl
from jax.experimental.pallas import tpu as pltpu
from jax.sharding import PartitionSpec as P

HD = 128
HEADS = 4
STRETCH = 256
ROWS = 512
KEYS = 1024
F32 = jnp.float32
BF16 = jnp.bfloat16
LOG2E = 1.4426950408889634
SCALE = HD ** (-0.5)
HIDDEN = -1e30


def dot(a, b, ca=1, cb=0):
    return lax.dot_general(a, b, (((ca,), (cb,)), ((), ())), preferred_element_type=F32)


def prepare(q_in, do_in, o_in, norm_in, qh, doh, qt, dot_, nb, dl, dqa):
    norm = norm_in[...] * LOG2E
    norm_cols = jnp.concatenate([norm, norm], axis=0).T
    for h in range(HEADS):
        rows = slice(h * ROWS, (h + 1) * ROWS)
        cols = slice(h * HD, (h + 1) * HD)
        q = q_in[:, cols]
        do = do_in[:, cols]
        qh[rows, :] = q
        doh[rows, :] = do
        qt[:, rows] = q.T
        dot_[:, rows] = do.T
        delta = jnp.sum(do.astype(F32) * o_in[:, cols].astype(F32), axis=1, keepdims=True)
        nb[rows, :] = jnp.broadcast_to(norm_cols[:, h : h + 1], (ROWS, HD))
        dl[rows, :] = jnp.broadcast_to(delta, (ROWS, HD))
    dqa[...] = jnp.zeros_like(dqa)


def step(k, v, kpos, qpos, qh, doh, qt, dot_, nb, dl, dqa, ps, dss):
    sub = 256
    for j in range(HEADS * ROWS // sub):
        rows = slice(j * sub, (j + 1) * sub)
        s = dot(qh[rows, :], k, 1, 1)
        dp = dot(doh[rows, :], v, 1, 1)
        seen = kpos <= qpos[j % 2]
        p = jnp.exp2(jnp.where(seen, s * (SCALE * LOG2E) - nb[rows, 0:1], HIDDEN))
        ds = (p * (dp - dl[rows, 0:1])).astype(BF16)
        ps[rows, :] = p.astype(BF16)
        dss[rows, :] = ds
        dqa[rows, :] += dot(ds, k)
    return dot(qt[...], dss[...]), dot(dot_[...], ps[...])


def kernel(q_in, do_in, o_in, norm_in, k_all, v_all, kpos_in, qpos_in, dq_out, term_out,
           qh, doh, qt, dot_, nb, dl, dqa, ps, dss):
    prepare(q_in, do_in, o_in, norm_in, qh, doh, qt, dot_, nb, dl, dqa)

    def body(i, _):
        ks = pl.ds(pl.multiple_of(i * KEYS, KEYS), KEYS)
        qpos = [qpos_in[0:STRETCH, 0:1], qpos_in[STRETCH:, 0:1]]
        dk, dv = step(k_all[ks, :], v_all[ks, :], kpos_in[0:1, ks], qpos,
                      qh, doh, qt, dot_, nb, dl, dqa, ps, dss)
        term_out[ks, 0:HD] = (dk * SCALE).astype(BF16).T
        term_out[ks, HD:] = dv.astype(BF16).T
        return 0

    lax.fori_loop(0, k_all.shape[0] // KEYS, body, 0)
    for h in range(HEADS):
        dq_out[:, h * HD : (h + 1) * HD] = (dqa[h * ROWS : (h + 1) * ROWS, :] * SCALE).astype(BF16)


def shards(queries, keys, values, outputs, out_grads, log_norms, stretch_order):
    me = lax.axis_index("ctx")
    key_all = lax.all_gather(keys, "ctx", axis=0, tiled=True)
    value_all = lax.all_gather(values, "ctx", axis=0, tiled=True)
    total = key_all.shape[0]
    pos = (stretch_order[:, None] * STRETCH + jnp.arange(STRETCH, dtype=jnp.int32)).reshape(-1)
    kpos = jnp.broadcast_to(pos[None, :], (8, total))
    qpos = lax.dynamic_slice_in_dim(pos, me * ROWS, ROWS, 0)
    qpos = jnp.broadcast_to(qpos[:, None], (ROWS, HD))
    rows = HEADS * ROWS
    vmem = pl.BlockSpec(memory_space=pltpu.VMEM)
    dq, term = pl.pallas_call(
        kernel,
        out_shape=[
            jax.ShapeDtypeStruct((ROWS, HEADS * HD), BF16),
            jax.ShapeDtypeStruct((total, 2 * HD), BF16),
        ],
        in_specs=[vmem] * 8,
        out_specs=[vmem] * 2,
        scratch_shapes=[
            pltpu.VMEM((rows, HD), BF16),
            pltpu.VMEM((rows, HD), BF16),
            pltpu.VMEM((HD, rows), BF16),
            pltpu.VMEM((HD, rows), BF16),
            pltpu.VMEM((rows, HD), F32),
            pltpu.VMEM((rows, HD), F32),
            pltpu.VMEM((rows, HD), F32),
            pltpu.VMEM((rows, KEYS), BF16),
            pltpu.VMEM((rows, KEYS), BF16),
        ],
        compiler_params=pltpu.CompilerParams(vmem_limit_bytes=58 * 2**20),
    )(queries, out_grads, outputs, log_norms, key_all, value_all, kpos, qpos)
    summed = lax.psum_scatter(term, "ctx", scatter_dimension=0, tiled=True)
    return dq, summed[:, :HD], summed[:, HD:]


def solution(mesh):
    return jax.shard_map(
        shards,
        mesh=mesh,
        in_specs=(
            P(("dp", "ctx"), "tp"),
            P(("dp", "ctx"), "tp"),
            P(("dp", "ctx"), "tp"),
            P(("dp", "ctx"), "tp"),
            P(("dp", "ctx"), "tp"),
            P("tp", ("dp", "ctx")),
            P("dp"),
        ),
        out_specs=(P(("dp", "ctx"), "tp"), P(("dp", "ctx"), "tp"), P(("dp", "ctx"), "tp")),
        check_vma=False,
    )
```

```python
import jax
import jax.numpy as jnp
from jax import lax
from jax.experimental import pallas as pl
from jax.experimental.pallas import tpu as pltpu
from jax.sharding import PartitionSpec as P

HD = 128
HEADS = 4
STRETCH = 256
ROWS = 512
KEYS = 1024
SUB = 256
SLOTS = 8
F32 = jnp.float32
BF16 = jnp.bfloat16
LOG2E = 1.4426950408889634
SCALE = HD ** (-0.5)
HIDDEN = -1e30
LO = pl.ds(0, ROWS)
HI = pl.ds(ROWS, ROWS)

S_O, S_PM, S_PM_SIB, S_XPM, S_XZ, S_XPM_SIB, S_XANDZ_SIB, S_XANDZ = range(SLOTS)


def dot(a, b, ca=1, cb=0):
    return lax.dot_general(a, b, (((ca,), (cb,)), ((), ())), preferred_element_type=F32)


def kernel(order, q_in, do_in, o_in, norm_in, k_in, v_in, dq_out, dk_out, dv_out,
           qh, doh, qt, dot_, nb, dl, dqa, ps, dss, kpos, qpos, kv, acc, stage,
           r_sib, r_in, comb, ssem, rsem):
    me = lax.axis_index("ctx")
    core = lax.rem(me, 2)
    chip = me // 2
    x = lax.rem(chip, 2)
    z = chip // 2
    zp, zm, z2 = lax.rem(z + 1, 4), lax.rem(z + 3, 4), lax.rem(z + 2, 4)

    def at(zz, xx, cc):
        return (zz * 2 + xx) * 2 + cc

    sib = at(z, x, 1 - core)
    across = at(z, 1 - x, core)
    up = at(zp, x, core)
    down = at(zm, x, core)
    far = at(z2, x, core)

    def copy(n, src, dst, where):
        return pltpu.make_async_remote_copy(
            src_ref=src, dst_ref=dst, send_sem=ssem.at[n], recv_sem=rsem.at[n],
            device_id={"ctx": where}, device_id_type=pl.DeviceIdType.MESH)

    half = ROWS // 2
    a_lo, a_hi = pl.ds(ROWS, half), pl.ds(ROWS + half, half)
    copies = [
        (kv.at[S_O, LO], kv.at[S_O, HI], sib),
        (kv.at[S_O, LO], kv.at[S_XANDZ, LO], across),
        (kv.at[S_O, LO], kv.at[S_PM, HI], up),
        (kv.at[S_O, LO], kv.at[S_PM, LO], down),
        (kv.at[S_PM, pl.ds(ROWS, half)], kv.at[S_XANDZ, a_lo], up),
        (kv.at[S_PM, pl.ds(half, half)], kv.at[S_XANDZ, a_hi], down),
        (kv.at[S_XANDZ, LO], kv.at[S_XPM, HI], up),
        (kv.at[S_XANDZ, LO], kv.at[S_XPM, LO], down),
        (kv.at[S_PM], kv.at[S_PM_SIB], sib),
        (kv.at[S_XANDZ, LO], kv.at[S_XANDZ_SIB, LO], sib),
        (kv.at[S_XANDZ, HI], kv.at[S_XANDZ_SIB, HI], sib),
        (kv.at[S_XANDZ, HI], kv.at[S_XZ, LO], across),
        (kv.at[S_XPM], kv.at[S_XPM_SIB], sib),
        (kv.at[S_XZ, LO], kv.at[S_XZ, HI], sib),
        (stage.at[S_O, 1], r_sib.at[0, 0], sib),
        (stage.at[S_PM_SIB], r_sib.at[1], sib),
        (stage.at[S_XZ, 1], r_sib.at[2, 0], sib),
        (stage.at[S_XPM_SIB], r_sib.at[3], sib),
        (stage.at[S_XANDZ_SIB], r_sib.at[4], sib),
        (comb.at[0], r_in.at[0], up),
        (comb.at[1], r_in.at[1], down),
        (comb.at[2], r_in.at[2], across),
        (comb.at[3], r_in.at[3], up),
        (comb.at[4], r_in.at[4], down),
        (comb.at[5], r_in.at[5], across),
        (comb.at[6], r_in.at[6], far),
    ]

    def start(*ns):
        for n in ns:
            copy(n, *copies[n]).start()

    def arrived(*ns):
        for n in ns:
            copy(n, *copies[n]).wait_recv()

    kv[S_O, 0:ROWS, 0:HD] = k_in[...]
    kv[S_O, 0:ROWS, HD:] = v_in[...]

    barrier = pltpu.get_barrier_semaphore()
    for other in (sib, across, up, down, far):
        pl.semaphore_signal(barrier, inc=1, device_id={"ctx": other},
                            device_id_type=pl.DeviceIdType.MESH)
    pl.semaphore_wait(barrier, 5)
    start(0, 1, 2, 3)

    row_iota = lax.broadcasted_iota(jnp.int32, (8, STRETCH), 1)
    col_iota = lax.broadcasted_iota(jnp.int32, (STRETCH, HD), 0)
    other_core = 1 - core
    other_x = 1 - x
    blocks = {
        S_O: (at(z, x, core), at(z, x, other_core)),
        S_PM: (at(zp, x, core), at(zm, x, core)),
        S_PM_SIB: (at(zp, x, other_core), at(zm, x, other_core)),
        S_XPM: (at(zp, other_x, core), at(zm, other_x, core)),
        S_XPM_SIB: (at(zp, other_x, other_core), at(zm, other_x, other_core)),
        S_XZ: (at(z2, other_x, core), at(z2, other_x, other_core)),
        S_XANDZ: (at(z, other_x, core), at(z2, x, core)),
        S_XANDZ_SIB: (at(z, other_x, other_core), at(z2, x, other_core)),
    }
    for s, owners in blocks.items():
        for b, owner in enumerate(owners):
            for t in range(2):
                c0 = b * ROWS + t * STRETCH
                kpos[s, :, c0 : c0 + STRETCH] = row_iota + order[owner * 2 + t] * STRETCH
    for t in range(2):
        qpos[t] = col_iota + order[me * 2 + t] * STRETCH

    norm = norm_in[...] * LOG2E
    norm_cols = jnp.concatenate([norm, norm], axis=0).T
    for h in range(HEADS):
        rows = slice(h * ROWS, (h + 1) * ROWS)
        cols = slice(h * HD, (h + 1) * HD)
        q = q_in[:, cols]
        do = do_in[:, cols]
        qh[rows, :] = q
        doh[rows, :] = do
        qt[:, rows] = q.T
        dot_[:, rows] = do.T
        delta = jnp.sum(do.astype(F32) * o_in[:, cols].astype(F32), axis=1, keepdims=True)
        nb[rows, :] = jnp.broadcast_to(norm_cols[:, h : h + 1], (ROWS, HD))
        dl[rows, :] = jnp.broadcast_to(delta, (ROWS, HD))
    dqa[...] = jnp.zeros_like(dqa)
    arrived(0)

    def rows_against(i, j):
        rows = slice(j * SUB, (j + 1) * SUB)
        k = kv[i, :, 0:HD]
        v = kv[i, :, HD:]
        s = dot(qh[rows, :], k, 1, 1)
        dp = dot(doh[rows, :], v, 1, 1)
        seen = kpos[i, 0:1, :] <= qpos[j % 2, :, 0:1]
        p = jnp.exp2(jnp.where(seen, s * (SCALE * LOG2E) - nb[rows, 0:1], HIDDEN))
        ds = (p * (dp - dl[rows, 0:1])).astype(BF16)
        ps[rows, :] = p.astype(BF16)
        dss[rows, :] = ds
        dqa[rows, :] += dot(ds, k)

    def combine(n, slot, part, sib_part, *arrivals):
        total = acc[slot, part] + sib_part[...].astype(F32)
        for r in arrivals:
            total += r_in[r].astype(F32)
        comb[n] = total.astype(BF16)

    def body(i, _):
        @pl.when(i == S_PM)
        def _():
            arrived(2, 3)
            start(4, 5, 8)
            arrived(1)
            start(6, 7, 9)

        @pl.when(i == S_PM_SIB)
        def _():
            arrived(8)
            arrived(4, 5)
            start(11, 10)

        @pl.when(i == S_XPM)
        def _():
            arrived(6, 7)
            start(12)

        @pl.when(i == S_XZ)
        def _():
            arrived(13)

        @pl.when(i == S_XPM_SIB)
        def _():
            arrived(12)

        @pl.when(i == S_XANDZ_SIB)
        def _():
            arrived(9, 10)

        for j in range(4):
            rows_against(i, j)

        @pl.when(i == S_XPM)
        def _():
            arrived(11)
            start(13)
            arrived(15)
            combine(0, S_PM, 0, r_sib.at[1, 0])
            combine(1, S_PM, 1, r_sib.at[1, 1])
            start(19, 20)

        @pl.when(i == S_XPM_SIB)
        def _():
            arrived(16)
            combine(2, S_XZ, 0, r_sib.at[2, 0])
            start(21)

        @pl.when(i == S_XANDZ_SIB)
        def _():
            arrived(17)
            combine(3, S_XPM, 0, r_sib.at[3, 0])
            combine(4, S_XPM, 1, r_sib.at[3, 1])
            start(22, 23)

        for j in range(4, 8):
            rows_against(i, j)
        dk = dot(qt[...], dss[...])
        dv = dot(dot_[...], ps[...])
        for part in range(2):
            cols = slice(part * ROWS, (part + 1) * ROWS)
            acc[i, part, 0:HD] = dk[:, cols]
            acc[i, part, HD:] = dv[:, cols]
            stage[i, part, 0:HD] = dk[:, cols].astype(BF16)
            stage[i, part, HD:] = dv[:, cols].astype(BF16)

        @pl.when(i == S_O)
        def _():
            start(14)

        @pl.when(i == S_PM_SIB)
        def _():
            start(15)

        @pl.when(i == S_XZ)
        def _():
            start(16)

        @pl.when(i == S_XPM_SIB)
        def _():
            start(17)

        @pl.when(i == S_XANDZ_SIB)
        def _():
            start(18)

        return 0

    lax.fori_loop(0, SLOTS, body, 0)
    arrived(18, 21)
    combine(6, S_XANDZ, 1, r_sib.at[4, 1], 2)
    start(25)
    arrived(22, 23)
    combine(5, S_XANDZ, 0, r_sib.at[4, 0], 3, 4)
    start(24)
    for h in range(HEADS):
        dq_out[:, h * HD : (h + 1) * HD] = (dqa[h * ROWS : (h + 1) * ROWS, :] * SCALE).astype(BF16)
    arrived(14, 19, 20)
    acc[S_O, 0] += r_sib[0, 0].astype(F32) + r_in[0].astype(F32) + r_in[1].astype(F32)
    arrived(24, 25)
    total = acc[S_O, 0] + r_in[5].astype(F32) + r_in[6].astype(F32)
    dk_out[...] = (total[0:HD] * SCALE).astype(BF16).T
    dv_out[...] = total[HD:].astype(BF16).T
    for n in range(len(copies)):
        copy(n, *copies[n]).wait_send()


def shards(queries, keys, values, outputs, out_grads, log_norms, stretch_order):
    rows = HEADS * ROWS
    vmem = pl.BlockSpec(memory_space=pltpu.VMEM)
    return pl.pallas_call(
        kernel,
        out_shape=[
            jax.ShapeDtypeStruct((ROWS, HEADS * HD), BF16),
            jax.ShapeDtypeStruct((ROWS, HD), BF16),
            jax.ShapeDtypeStruct((ROWS, HD), BF16),
        ],
        in_specs=[pl.BlockSpec(memory_space=pltpu.SMEM)] + [vmem] * 6,
        out_specs=[vmem] * 3,
        scratch_shapes=[
            pltpu.VMEM((rows, HD), BF16),
            pltpu.VMEM((rows, HD), BF16),
            pltpu.VMEM((HD, rows), BF16),
            pltpu.VMEM((HD, rows), BF16),
            pltpu.VMEM((rows, HD), F32),
            pltpu.VMEM((rows, HD), F32),
            pltpu.VMEM((rows, HD), F32),
            pltpu.VMEM((rows, KEYS), BF16),
            pltpu.VMEM((rows, KEYS), BF16),
            pltpu.VMEM((SLOTS, 8, KEYS), jnp.int32),
            pltpu.VMEM((2, STRETCH, HD), jnp.int32),
            pltpu.VMEM((SLOTS, KEYS, 2 * HD), BF16),
            pltpu.VMEM((SLOTS, 2, 2 * HD, ROWS), F32),
            pltpu.VMEM((SLOTS, 2, 2 * HD, ROWS), BF16),
            pltpu.VMEM((5, 2, 2 * HD, ROWS), BF16),
            pltpu.VMEM((7, 2 * HD, ROWS), BF16),
            pltpu.VMEM((7, 2 * HD, ROWS), BF16),
            pltpu.SemaphoreType.DMA((26,)),
            pltpu.SemaphoreType.DMA((26,)),
        ],
        compiler_params=pltpu.CompilerParams(
            vmem_limit_bytes=58 * 2**20, collective_id=0, has_side_effects=True
        ),
    )(stretch_order, queries, out_grads, outputs, log_norms, keys, values)


def solution(mesh):
    return jax.shard_map(
        shards,
        mesh=mesh,
        in_specs=(
            P(("dp", "ctx"), "tp"),
            P(("dp", "ctx"), "tp"),
            P(("dp", "ctx"), "tp"),
            P(("dp", "ctx"), "tp"),
            P(("dp", "ctx"), "tp"),
            P("tp", ("dp", "ctx")),
            P("dp"),
        ),
        out_specs=(P(("dp", "ctx"), "tp"), P(("dp", "ctx"), "tp"), P(("dp", "ctx"), "tp")),
        check_vma=False,
    )
```

```python
import jax
import jax.numpy as jnp
from jax import lax
from jax.experimental import pallas as pl
from jax.experimental.pallas import tpu as pltpu
from jax.sharding import PartitionSpec as P

HD = 128
HEADS = 4
STRETCH = 256
ROWS = 512
KEYS = 1024
SUB = 256
SLOTS = 8
HALF = 1024
F32 = jnp.float32
BF16 = jnp.bfloat16
LOG2E = 1.4426950408889634
SCALE = HD ** (-0.5)
HIDDEN = -1e30
LO = pl.ds(0, ROWS)
HI = pl.ds(ROWS, ROWS)

S_O, S_PM, S_PM_SIB, S_XPM, S_XZ, S_XPM_SIB, S_XANDZ_SIB, S_XANDZ = range(SLOTS)


def dot(a, b, ca=1, cb=0):
    return lax.dot_general(a, b, (((ca,), (cb,)), ((), ())), preferred_element_type=F32)


def kernel(order, q_in, do_in, o_in, norm_in, k_in, v_in, dq_out, dk_out, dv_out,
           qh, doh, oh, qt, dot_, nb, dl, dqa, ps, dss, kpos, qpos, kv, acc, stage,
           r_sib, r_in, comb, dqb, dkb, dvb, ssem, rsem, isem, osem):
    me = lax.axis_index("ctx")
    core = lax.rem(me, 2)
    chip = me // 2
    x = lax.rem(chip, 2)
    z = chip // 2
    zp, zm, z2 = lax.rem(z + 1, 4), lax.rem(z + 3, 4), lax.rem(z + 2, 4)

    def at(zz, xx, cc):
        return (zz * 2 + xx) * 2 + cc

    sib = at(z, x, 1 - core)
    across = at(z, 1 - x, core)
    up = at(zp, x, core)
    down = at(zm, x, core)
    far = at(z2, x, core)

    def copy(n, src, dst, where):
        return pltpu.make_async_remote_copy(
            src_ref=src, dst_ref=dst, send_sem=ssem.at[n], recv_sem=rsem.at[n],
            device_id={"ctx": where}, device_id_type=pl.DeviceIdType.MESH)

    half = ROWS // 2
    a_lo, a_hi = pl.ds(ROWS, half), pl.ds(ROWS + half, half)
    copies = [
        (kv.at[S_O, LO], kv.at[S_O, HI], sib),
        (kv.at[S_O, LO], kv.at[S_XANDZ, LO], across),
        (kv.at[S_O, LO], kv.at[S_PM, HI], up),
        (kv.at[S_O, LO], kv.at[S_PM, LO], down),
        (kv.at[S_PM, pl.ds(ROWS, half)], kv.at[S_XANDZ, a_lo], up),
        (kv.at[S_PM, pl.ds(half, half)], kv.at[S_XANDZ, a_hi], down),
        (kv.at[S_XANDZ, LO], kv.at[S_XPM, HI], up),
        (kv.at[S_XANDZ, LO], kv.at[S_XPM, LO], down),
        (kv.at[S_PM], kv.at[S_PM_SIB], sib),
        (kv.at[S_XANDZ, LO], kv.at[S_XANDZ_SIB, LO], sib),
        (kv.at[S_XANDZ, HI], kv.at[S_XANDZ_SIB, HI], sib),
        (kv.at[S_XANDZ, HI], kv.at[S_XZ, LO], across),
        (kv.at[S_XPM], kv.at[S_XPM_SIB], sib),
        (kv.at[S_XZ, LO], kv.at[S_XZ, HI], sib),
        (stage.at[S_O, 1], r_sib.at[0, 0], sib),
        (stage.at[S_PM_SIB], r_sib.at[1], sib),
        (stage.at[S_XZ, 1], r_sib.at[2, 0], sib),
        (stage.at[S_XPM_SIB], r_sib.at[3], sib),
        (stage.at[S_XANDZ_SIB], r_sib.at[4], sib),
        (comb.at[0], r_in.at[0], up),
        (comb.at[1], r_in.at[1], down),
        (comb.at[2], r_in.at[2], across),
        (comb.at[3], r_in.at[3], up),
        (comb.at[4], r_in.at[4], down),
        (comb.at[5], r_in.at[5], across),
        (comb.at[6], r_in.at[6], far),
    ]

    def start(*ns):
        for n in ns:
            copy(n, *copies[n]).start()

    def arrived(*ns):
        for n in ns:
            copy(n, *copies[n]).wait_recv()

    barrier = pltpu.get_barrier_semaphore()
    for other in (sib, across, up, down, far):
        pl.semaphore_signal(barrier, inc=1, device_id={"ctx": other},
                            device_id_type=pl.DeviceIdType.MESH)
    loads = [(k_in, kv.at[S_O, LO, pl.ds(0, HD)]), (v_in, kv.at[S_O, LO, pl.ds(HD, HD)])]
    for h in range(HEADS):
        cols, rows = pl.ds(h * HD, HD), pl.ds(h * ROWS, ROWS)
        loads += [(q_in.at[:, cols], qh.at[rows]), (do_in.at[:, cols], doh.at[rows]),
                  (o_in.at[:, cols], oh.at[rows])]
    loads = [pltpu.make_async_copy(src, dst, isem.at[n]) for n, (src, dst) in enumerate(loads)]
    for load in loads:
        load.start()
    loads[0].wait()
    loads[1].wait()
    pl.semaphore_wait(barrier, 5)
    start(0, 1, 2, 3)
    acc[...] = jnp.zeros_like(acc)
    dqa[...] = jnp.zeros_like(dqa)

    row_iota = lax.broadcasted_iota(jnp.int32, (8, STRETCH), 1)
    col_iota = lax.broadcasted_iota(jnp.int32, (STRETCH, HD), 0)
    other_core = 1 - core
    other_x = 1 - x
    blocks = {
        S_O: (at(z, x, core), at(z, x, other_core)),
        S_PM: (at(zp, x, core), at(zm, x, core)),
        S_PM_SIB: (at(zp, x, other_core), at(zm, x, other_core)),
        S_XPM: (at(zp, other_x, core), at(zm, other_x, core)),
        S_XPM_SIB: (at(zp, other_x, other_core), at(zm, other_x, other_core)),
        S_XZ: (at(z2, other_x, core), at(z2, other_x, other_core)),
        S_XANDZ: (at(z, other_x, core), at(z2, x, core)),
        S_XANDZ_SIB: (at(z, other_x, other_core), at(z2, x, other_core)),
    }
    for s, owners in blocks.items():
        for b, owner in enumerate(owners):
            for t in range(2):
                c0 = b * ROWS + t * STRETCH
                kpos[s, :, c0 : c0 + STRETCH] = row_iota + order[owner * 2 + t] * STRETCH
    for t in range(2):
        qpos[t] = col_iota + order[me * 2 + t] * STRETCH

    norm = norm_in[...] * LOG2E
    norm_cols = jnp.concatenate([norm, norm], axis=0).T
    for load in loads[2:]:
        load.wait()
    for h in range(HEADS):
        rows = slice(h * ROWS, (h + 1) * ROWS)
        do = doh[rows, :]
        qt[:, rows] = qh[rows, :].T
        dot_[:, rows] = do.T
        delta = jnp.sum(do.astype(F32) * oh[rows, :].astype(F32), axis=1, keepdims=True)
        nb[rows, :] = jnp.broadcast_to(norm_cols[:, h : h + 1], (ROWS, HD))
        dl[rows, :] = jnp.broadcast_to(delta, (ROWS, HD))
    arrived(0)

    def wide(a):
        return jnp.concatenate([a] * (KEYS // HD), axis=1)

    def compute(slot, row0):
        for j in range(HALF // SUB):
            rows = pl.ds(pl.multiple_of(row0 + j * SUB, SUB), SUB)
            part_rows = slice(j * SUB, (j + 1) * SUB)
            k = kv[slot, :, 0:HD]
            v = kv[slot, :, HD:]
            s = dot(qh[rows, :], k, 1, 1)
            dp = dot(doh[rows, :], v, 1, 1)
            seen = kpos[slot, 0:1, :] <= wide(qpos[j % 2])
            p = jnp.exp2(jnp.where(seen, s * (SCALE * LOG2E) - wide(nb[rows, :]), HIDDEN))
            ds = (p * (dp - wide(dl[rows, :]))).astype(BF16)
            ps[part_rows, :] = p.astype(BF16)
            dss[part_rows, :] = ds
            dqa[rows, :] += dot(ds, k)
        rows = pl.ds(pl.multiple_of(row0, HALF), HALF)
        dk = dot(qt[:, rows], dss[...])
        dv = dot(dot_[:, rows], ps[...])
        for part in range(2):
            cols = slice(part * ROWS, (part + 1) * ROWS)
            dk_sum = acc[slot, part, 0:HD] + dk[:, cols]
            dv_sum = acc[slot, part, HD:] + dv[:, cols]
            acc[slot, part, 0:HD] = dk_sum
            acc[slot, part, HD:] = dv_sum
            stage[slot, part, 0:HD] = dk_sum.astype(BF16)
            stage[slot, part, HD:] = dv_sum.astype(BF16)

    def combine(n, slot, part, sib_part, *arrivals):
        total = acc[slot, part] + sib_part[...].astype(F32)
        for r in arrivals:
            total += r_in[r].astype(F32)
        comb[n] = total.astype(BF16)

    def body(t, _):
        @pl.when(t == 1)
        def _():
            arrived(2, 3)
            start(4, 5, 8)
            arrived(1)
            start(6, 7, 9)

        @pl.when(t == 3)
        def _():
            arrived(8)
            arrived(4, 5)
            start(11, 10)

        @pl.when(t == 5)
        def _():
            start(15)
            arrived(6, 7)
            start(12)

        @pl.when(t == 6)
        def _():
            arrived(11)
            start(13)
            arrived(15)
            combine(0, S_PM, 0, r_sib.at[1, 0])
            combine(1, S_PM, 1, r_sib.at[1, 1])
            start(19, 20)

        @pl.when(t == 7)
        def _():
            arrived(13)

        @pl.when(t == 9)
        def _():
            start(16)
            arrived(12)

        @pl.when(t == 10)
        def _():
            arrived(16)
            combine(2, S_XZ, 0, r_sib.at[2, 0])
            start(21)

        @pl.when(t == 11)
        def _():
            start(17)
            arrived(9, 10)

        @pl.when(t == 12)
        def _():
            arrived(17)
            combine(3, S_XPM, 0, r_sib.at[3, 0])
            combine(4, S_XPM, 1, r_sib.at[3, 1])
            start(22, 23)

        @pl.when(t == 13)
        def _():
            start(18)

        @pl.when(t == 15)
        def _():
            arrived(18, 21)
            combine(6, S_XANDZ, 1, r_sib.at[4, 1], 2)
            start(25)
            arrived(22, 23)
            combine(5, S_XANDZ, 0, r_sib.at[4, 0], 3, 4)
            start(24)

        compute(lax.rem((t + 1) // 2, SLOTS), lax.rem(t + 1, 2) * HALF)
        return 0

    lax.fori_loop(0, 2 * SLOTS, body, 0)
    start(14)
    outs = []
    for h in range(HEADS):
        cols = slice(h * HD, (h + 1) * HD)
        dqb[:, cols] = (dqa[h * ROWS : (h + 1) * ROWS, :] * SCALE).astype(BF16)
    outs.append(pltpu.make_async_copy(dqb, dq_out, osem.at[0]))
    outs[0].start()
    arrived(19, 20, 14)
    acc[S_O, 0] += r_sib[0, 0].astype(F32) + r_in[0].astype(F32) + r_in[1].astype(F32)
    arrived(24, 25)
    total = acc[S_O, 0] + r_in[5].astype(F32) + r_in[6].astype(F32)
    dkb[...] = (total[0:HD] * SCALE).astype(BF16).T
    dvb[...] = total[HD:].astype(BF16).T
    outs.append(pltpu.make_async_copy(dkb, dk_out, osem.at[1]))
    outs.append(pltpu.make_async_copy(dvb, dv_out, osem.at[2]))
    outs[1].start()
    outs[2].start()
    for n in range(len(copies)):
        copy(n, *copies[n]).wait_send()
    for out in outs:
        out.wait()


def hand_over(dq, dk, dv, dq_out, dk_out, dv_out):
    dq_out[...] = dq[...]
    dk_out[...] = dk[...]
    dv_out[...] = dv[...]


def shards(queries, keys, values, outputs, out_grads, log_norms, stretch_order):
    rows = HEADS * ROWS
    anywhere = pl.BlockSpec(memory_space=pl.ANY)
    shapes = [
        jax.ShapeDtypeStruct((ROWS, HEADS * HD), BF16),
        jax.ShapeDtypeStruct((ROWS, HD), BF16),
        jax.ShapeDtypeStruct((ROWS, HD), BF16),
    ]
    grads = pl.pallas_call(
        kernel,
        out_shape=shapes,
        in_specs=[pl.BlockSpec(memory_space=pltpu.SMEM), anywhere, anywhere, anywhere,
                  pl.BlockSpec(memory_space=pltpu.VMEM), anywhere, anywhere],
        out_specs=[anywhere] * 3,
        scratch_shapes=[
            pltpu.VMEM((rows, HD), BF16),
            pltpu.VMEM((rows, HD), BF16),
            pltpu.VMEM((rows, HD), BF16),
            pltpu.VMEM((HD, rows), BF16),
            pltpu.VMEM((HD, rows), BF16),
            pltpu.VMEM((rows, HD), F32),
            pltpu.VMEM((rows, HD), F32),
            pltpu.VMEM((rows, HD), F32),
            pltpu.VMEM((HALF, KEYS), BF16),
            pltpu.VMEM((HALF, KEYS), BF16),
            pltpu.VMEM((SLOTS, 8, KEYS), jnp.int32),
            pltpu.VMEM((2, STRETCH, HD), jnp.int32),
            pltpu.VMEM((SLOTS, KEYS, 2 * HD), BF16),
            pltpu.VMEM((SLOTS, 2, 2 * HD, ROWS), F32),
            pltpu.VMEM((SLOTS, 2, 2 * HD, ROWS), BF16),
            pltpu.VMEM((5, 2, 2 * HD, ROWS), BF16),
            pltpu.VMEM((7, 2 * HD, ROWS), BF16),
            pltpu.VMEM((7, 2 * HD, ROWS), BF16),
            pltpu.VMEM((ROWS, HEADS * HD), BF16),
            pltpu.VMEM((ROWS, HD), BF16),
            pltpu.VMEM((ROWS, HD), BF16),
            pltpu.SemaphoreType.DMA((26,)),
            pltpu.SemaphoreType.DMA((26,)),
            pltpu.SemaphoreType.DMA((14,)),
            pltpu.SemaphoreType.DMA((3,)),
        ],
        compiler_params=pltpu.CompilerParams(
            vmem_limit_bytes=58 * 2**20, collective_id=0, has_side_effects=True
        ),
    )(stretch_order, queries, out_grads, outputs, log_norms, keys, values)
    return pl.pallas_call(
        hand_over,
        out_shape=shapes,
        in_specs=[pl.BlockSpec(memory_space=pltpu.VMEM)] * 3,
        out_specs=[pl.BlockSpec(memory_space=pltpu.VMEM)] * 3,
    )(*grads)


def solution(mesh):
    return jax.shard_map(
        shards,
        mesh=mesh,
        in_specs=(
            P(("dp", "ctx"), "tp"),
            P(("dp", "ctx"), "tp"),
            P(("dp", "ctx"), "tp"),
            P(("dp", "ctx"), "tp"),
            P(("dp", "ctx"), "tp"),
            P("tp", ("dp", "ctx")),
            P("dp"),
        ),
        out_specs=(P(("dp", "ctx"), "tp"), P(("dp", "ctx"), "tp"), P(("dp", "ctx"), "tp")),
        check_vma=False,
    )
```

```python
import jax
import jax.numpy as jnp
from jax import lax
from jax.experimental import pallas as pl
from jax.experimental.pallas import tpu as pltpu
from jax.sharding import PartitionSpec

HD = 128
HEADS = 4
STRETCH = 256
ROWS = 512
KEYS = 512
STEPS = 16
F32 = jnp.float32
BF16 = jnp.bfloat16
LOG2E = 1.4426950408889634
SCALE = HD ** (-0.5)
HIDDEN = -1e30
FIRST = pl.ds(0, STRETCH)
SECOND = pl.ds(STRETCH, STRETCH)
HALVES = (FIRST, SECOND)

O, P0, P1, P0S, P1S, R0, R1, R0S, XZ, XZS, R1S, Q0S, Q1S, Q0, Q1, OS = range(STEPS)
P, PS, R, RS, Q, QS = (P0, P1), (P0S, P1S), (R0, R1), (R0S, R1S), (Q0, Q1), (Q0S, Q1S)


def dot(a, b, ca=1, cb=0):
    return lax.dot_general(a, b, (((ca,), (cb,)), ((), ())), preferred_element_type=F32)


def kernel(order, q_in, do_in, o_in, norm_in, k_in, v_in, dq_out, dk_out, dv_out,
           qh, doh, oh, qt, dot_, nb, dl, dqa, ps, dss, kpos, qpos, kv, acc, stage,
           r_sib, r_in, comb, r_xz, comb_xz, dqb, dkb, dvb, ssem, rsem, isem, osem):
    me = lax.axis_index("ctx")
    core = lax.rem(me, 2)
    chip = me // 2
    x = lax.rem(chip, 2)
    z = chip // 2
    zp, zm, z2 = lax.rem(z + 1, 4), lax.rem(z + 3, 4), lax.rem(z + 2, 4)

    def at(zz, xx, cc):
        return (zz * 2 + xx) * 2 + cc

    sib = at(z, x, 1 - core)
    across = at(z, 1 - x, core)
    up = at(zp, x, core)
    down = at(zm, x, core)
    far = at(z2, x, core)

    def copy(n, src, dst, where):
        return pltpu.make_async_remote_copy(
            src_ref=src, dst_ref=dst, send_sem=ssem.at[n], recv_sem=rsem.at[n],
            device_id={"ctx": where}, device_id_type=pl.DeviceIdType.MESH)

    copies = {"o": (kv.at[O], kv.at[OS], sib), "xz": (kv.at[XZ], kv.at[XZS], sib),
              "x2": (comb_xz, r_xz, across), "os": (stage.at[OS], r_sib.at[0], sib),
              "xzs": (stage.at[XZS], r_sib.at[5], sib),
              "z0": (kv.at[P0, SECOND], kv.at[Q0, SECOND], up),
              "z1": (kv.at[P1, FIRST], kv.at[Q1, SECOND], down)}
    for h in range(2):
        own = kv.at[O, HALVES[h]]
        copies |= {
            f"ou{h}": (own, kv.at[P[h], SECOND], up),
            f"od{h}": (own, kv.at[P[h], FIRST], down),
            f"ox{h}": (own, kv.at[Q[h], FIRST], across),
            f"xu{h}": (kv.at[Q[h], FIRST], kv.at[R[h], SECOND], up),
            f"xd{h}": (kv.at[Q[h], FIRST], kv.at[R[h], FIRST], down),
            f"zx{h}": (kv.at[Q[h], SECOND], kv.at[XZ, HALVES[h]], across),
            f"p{h}": (kv.at[P[h]], kv.at[PS[h]], sib),
            f"q{h}": (kv.at[Q[h]], kv.at[QS[h]], sib),
            f"r{h}": (kv.at[R[h]], kv.at[RS[h]], sib),
            f"ps{h}": (stage.at[PS[h]], r_sib.at[1 + h], sib),
            f"rs{h}": (stage.at[RS[h]], r_sib.at[3 + h], sib),
            f"qs{h}": (stage.at[QS[h]], r_sib.at[6 + h], sib),
            f"pu{h}": (comb.at[h, 0], r_in.at[h, 0], up),
            f"pd{h}": (comb.at[h, 1], r_in.at[h, 1], down),
            f"ru{h}": (comb.at[2 + h, 0], r_in.at[2 + h, 0], up),
            f"rd{h}": (comb.at[2 + h, 1], r_in.at[2 + h, 1], down),
            f"qx{h}": (comb.at[4 + h, 0], r_in.at[4 + h, 0], across),
            f"qz{h}": (comb.at[4 + h, 1], r_in.at[4 + h, 1], far),
        }
    number = {name: n for n, name in enumerate(copies)}

    def start(names):
        for name in names.split():
            copy(number[name], *copies[name]).start()

    def arrived(names):
        for name in names.split():
            copy(number[name], *copies[name]).wait_recv()

    barrier = pltpu.get_barrier_semaphore()
    for other in (sib, across, up, down, far):
        pl.semaphore_signal(barrier, inc=1, device_id={"ctx": other},
                            device_id_type=pl.DeviceIdType.MESH)
    loads = [(k_in, kv.at[O, :, pl.ds(0, HD)]), (v_in, kv.at[O, :, pl.ds(HD, HD)])]
    for h in range(HEADS):
        cols, rows = pl.ds(h * HD, HD), pl.ds(h * ROWS, ROWS)
        loads += [(q_in.at[:, cols], qh.at[rows]), (do_in.at[:, cols], doh.at[rows]),
                  (o_in.at[:, cols], oh.at[rows])]
    loads = [pltpu.make_async_copy(src, dst, isem.at[n]) for n, (src, dst) in enumerate(loads)]
    for load in loads:
        load.start()
    loads[0].wait()
    loads[1].wait()
    pl.semaphore_wait(barrier, 5)
    start("ou0 od0 ox0 ou1 od1 ox1 o")
    dqa[...] = jnp.zeros_like(dqa)

    row_iota = lax.broadcasted_iota(jnp.int32, (8, STRETCH), 1)
    col_iota = lax.broadcasted_iota(jnp.int32, (STRETCH, HD), 0)
    other_core = 1 - core
    other_x = 1 - x
    blocks = {O: (me * 2, me * 2 + 1), OS: (sib * 2, sib * 2 + 1)}
    blocks[XZ] = tuple(at(z2, other_x, core) * 2 + h for h in range(2))
    blocks[XZS] = tuple(at(z2, other_x, other_core) * 2 + h for h in range(2))
    for h in range(2):
        for block, c in ((P[h], core), (PS[h], other_core)):
            blocks[block] = (at(zp, x, c) * 2 + h, at(zm, x, c) * 2 + h)
        for block, c in ((R[h], core), (RS[h], other_core)):
            blocks[block] = (at(zp, other_x, c) * 2 + h, at(zm, other_x, c) * 2 + h)
        for block, c in ((Q[h], core), (QS[h], other_core)):
            blocks[block] = (at(z, other_x, c) * 2 + h, at(z2, x, c) * 2 + h)
    for block, stretches in blocks.items():
        for h, stretch in enumerate(stretches):
            cols = slice(h * STRETCH, (h + 1) * STRETCH)
            kpos[block, :, cols] = row_iota + order[stretch] * STRETCH
    for h in range(2):
        qpos[h * STRETCH : (h + 1) * STRETCH] = col_iota + order[me * 2 + h] * STRETCH

    norm = norm_in[...] * LOG2E
    norm_cols = jnp.concatenate([norm, norm], axis=0).T
    for load in loads[2:]:
        load.wait()
    for h in range(HEADS):
        rows = slice(h * ROWS, (h + 1) * ROWS)
        do = doh[rows, :]
        qt[:, rows] = qh[rows, :].T
        dot_[:, rows] = do.T
        delta = jnp.sum(do.astype(F32) * oh[rows, :].astype(F32), axis=1, keepdims=True)
        nb[rows, :] = jnp.broadcast_to(norm_cols[:, h : h + 1], (ROWS, HD))
        dl[rows, :] = jnp.broadcast_to(delta, (ROWS, HD))

    def wide(a):
        return jnp.concatenate([a] * (KEYS // HD), axis=1)

    def compute(b):
        for h in range(HEADS):
            rows = slice(h * ROWS, (h + 1) * ROWS)
            k = kv[b, :, 0:HD]
            v = kv[b, :, HD:]
            s = dot(qh[rows, :], k, 1, 1)
            dp = dot(doh[rows, :], v, 1, 1)
            seen = kpos[b, 0:1, :] <= wide(qpos[...])
            p = jnp.exp2(jnp.where(seen, s * (SCALE * LOG2E) - wide(nb[rows, :]), HIDDEN))
            ds = (p * (dp - wide(dl[rows, :]))).astype(BF16)
            ps[rows, :] = p.astype(BF16)
            dss[rows, :] = ds
            dqa[rows, :] += dot(ds, k)
        dk = dot(qt[...], dss[...])
        dv = dot(dot_[...], ps[...])
        acc[b, 0:HD] = dk
        acc[b, HD:] = dv
        stage[b, 0:HD] = dk.astype(BF16)
        stage[b, HD:] = dv.astype(BF16)

    def combine(n, block, sib_part):
        total = acc[block] + r_sib[sib_part].astype(F32)
        for part in range(2):
            cols = slice(part * STRETCH, (part + 1) * STRETCH)
            comb[n, part] = total[:, cols].astype(BF16)

    def combine_q(h):
        cols = slice(h * STRETCH, (h + 1) * STRETCH)
        total = acc[Q[h]] + r_sib[6 + h].astype(F32)
        comb[4 + h, 0] = (total[:, :STRETCH] + r_in[2 + h, 0].astype(F32)
                          + r_in[2 + h, 1].astype(F32)).astype(BF16)
        comb[4 + h, 1] = (total[:, STRETCH:] + r_xz[:, cols].astype(F32)).astype(BF16)

    def before(t):
        if t == P0:
            arrived("ou0 od0")
            start("z0 p0")
            arrived("ox0")
            start("xd0")
        if t == P1:
            arrived("ou1 od1")
            start("z1 xu0 p1")
        if t == P0S:
            arrived("ox1")
            start("xu1 xd1")
            arrived("p0")
        if t == P1S:
            start("ps0")
            arrived("p1 z0 z1")
            start("zx0 zx1 q0 q1")
        if t == R0:
            start("ps1")
            arrived("xu0 xd0")
            start("r0")
            arrived("ps0")
            combine(0, P0, 1)
            start("pu0 pd0")
        if t == R1:
            arrived("xu1 xd1")
            start("r1")
            arrived("ps1")
            combine(1, P1, 2)
            start("pu1 pd1")
        if t == R0S:
            arrived("r0")
        if t == XZ:
            start("rs0")
            arrived("zx0 zx1")
            start("xz")
        if t == XZS:
            arrived("xz rs0")
            combine(2, R0, 3)
            start("ru0 rd0")
        if t == R1S:
            start("xzs")
            arrived("r1")
        if t == Q0S:
            start("rs1")
            arrived("xzs")
            comb_xz[...] = (acc[XZ] + r_sib[5].astype(F32)).astype(BF16)
            start("x2")
            arrived("q0")
        if t == Q1S:
            start("qs0")
            arrived("rs1")
            combine(3, R1, 4)
            start("ru1 rd1")
            arrived("q1")
        if t == Q0:
            start("qs1")
        if t == Q1:
            arrived("qs0 ru0 rd0 x2")
            combine_q(0)
            start("qx0 qz0")
        if t == OS:
            arrived("qs1 ru1 rd1")
            combine_q(1)
            start("qx1 qz1")
            arrived("o")

    def body(t, _):
        for n in range(1, STEPS):
            pl.when(t == n)(lambda n=n: before(n))
        compute(t)
        return 0

    lax.fori_loop(0, STEPS, body, 0)
    start("os")
    outs = []
    for h in range(HEADS):
        cols = slice(h * HD, (h + 1) * HD)
        dqb[:, cols] = (dqa[h * ROWS : (h + 1) * ROWS, :] * SCALE).astype(BF16)
    outs.append(pltpu.make_async_copy(dqb, dq_out, osem.at[0]))
    outs[0].start()
    arrived("os pu0 pd0 pu1 pd1")
    for h in range(2):
        cols = slice(h * STRETCH, (h + 1) * STRETCH)
        acc[O, :, cols] += (r_sib[0, :, cols].astype(F32) + r_in[h, 0].astype(F32)
                            + r_in[h, 1].astype(F32))
    arrived("qx0 qz0")
    acc[O, :, 0:STRETCH] += r_in[4, 0].astype(F32) + r_in[4, 1].astype(F32)
    arrived("qx1 qz1")
    acc[O, :, STRETCH:] += r_in[5, 0].astype(F32) + r_in[5, 1].astype(F32)
    total = acc[O]
    dkb[...] = (total[0:HD] * SCALE).astype(BF16).T
    dvb[...] = total[HD:].astype(BF16).T
    outs.append(pltpu.make_async_copy(dkb, dk_out, osem.at[1]))
    outs.append(pltpu.make_async_copy(dvb, dv_out, osem.at[2]))
    outs[1].start()
    outs[2].start()
    for name in copies:
        copy(number[name], *copies[name]).wait_send()
    for out in outs:
        out.wait()


def hand_over(dq, dk, dv, dq_out, dk_out, dv_out):
    dq_out[...] = dq[...]
    dk_out[...] = dk[...]
    dv_out[...] = dv[...]


def shards(queries, keys, values, outputs, out_grads, log_norms, stretch_order):
    rows = HEADS * ROWS
    anywhere = pl.BlockSpec(memory_space=pl.ANY)
    shapes = [
        jax.ShapeDtypeStruct((ROWS, HEADS * HD), BF16),
        jax.ShapeDtypeStruct((ROWS, HD), BF16),
        jax.ShapeDtypeStruct((ROWS, HD), BF16),
    ]
    grads = pl.pallas_call(
        kernel,
        out_shape=shapes,
        in_specs=[pl.BlockSpec(memory_space=pltpu.SMEM), anywhere, anywhere, anywhere,
                  pl.BlockSpec(memory_space=pltpu.VMEM), anywhere, anywhere],
        out_specs=[anywhere] * 3,
        scratch_shapes=[
            pltpu.VMEM((rows, HD), BF16),
            pltpu.VMEM((rows, HD), BF16),
            pltpu.VMEM((rows, HD), BF16),
            pltpu.VMEM((HD, rows), BF16),
            pltpu.VMEM((HD, rows), BF16),
            pltpu.VMEM((rows, HD), F32),
            pltpu.VMEM((rows, HD), F32),
            pltpu.VMEM((rows, HD), F32),
            pltpu.VMEM((rows, KEYS), BF16),
            pltpu.VMEM((rows, KEYS), BF16),
            pltpu.VMEM((STEPS, 8, KEYS), jnp.int32),
            pltpu.VMEM((ROWS, HD), jnp.int32),
            pltpu.VMEM((STEPS, KEYS, 2 * HD), BF16),
            pltpu.VMEM((STEPS, 2 * HD, KEYS), F32),
            pltpu.VMEM((STEPS, 2 * HD, KEYS), BF16),
            pltpu.VMEM((8, 2 * HD, KEYS), BF16),
            pltpu.VMEM((6, 2, 2 * HD, STRETCH), BF16),
            pltpu.VMEM((6, 2, 2 * HD, STRETCH), BF16),
            pltpu.VMEM((2 * HD, KEYS), BF16),
            pltpu.VMEM((2 * HD, KEYS), BF16),
            pltpu.VMEM((ROWS, HEADS * HD), BF16),
            pltpu.VMEM((ROWS, HD), BF16),
            pltpu.VMEM((ROWS, HD), BF16),
            pltpu.SemaphoreType.DMA((43,)),
            pltpu.SemaphoreType.DMA((43,)),
            pltpu.SemaphoreType.DMA((14,)),
            pltpu.SemaphoreType.DMA((3,)),
        ],
        compiler_params=pltpu.CompilerParams(
            vmem_limit_bytes=58 * 2**20, collective_id=0, has_side_effects=True
        ),
    )(stretch_order, queries, out_grads, outputs, log_norms, keys, values)
    return pl.pallas_call(
        hand_over,
        out_shape=shapes,
        in_specs=[pl.BlockSpec(memory_space=pltpu.VMEM)] * 3,
        out_specs=[pl.BlockSpec(memory_space=pltpu.VMEM)] * 3,
    )(*grads)


def solution(mesh):
    return jax.shard_map(
        shards,
        mesh=mesh,
        in_specs=(
            PartitionSpec(("dp", "ctx"), "tp"),
            PartitionSpec(("dp", "ctx"), "tp"),
            PartitionSpec(("dp", "ctx"), "tp"),
            PartitionSpec(("dp", "ctx"), "tp"),
            PartitionSpec(("dp", "ctx"), "tp"),
            PartitionSpec("tp", ("dp", "ctx")),
            PartitionSpec("dp"),
        ),
        out_specs=(PartitionSpec(("dp", "ctx"), "tp"), PartitionSpec(("dp", "ctx"), "tp"), PartitionSpec(("dp", "ctx"), "tp")),
        check_vma=False,
    )
```

```python
import jax
import jax.numpy as jnp
from jax import lax
from jax.experimental import pallas as pl
from jax.experimental.pallas import tpu as pltpu
from jax.sharding import PartitionSpec

HD = 128
HEADS = 4
STRETCH = 256
ROWS = 512
KEYS = 512
STEPS = 16
F32 = jnp.float32
BF16 = jnp.bfloat16
LOG2E = 1.4426950408889634
SCALE = HD ** (-0.5)
HIDDEN = -1e30
FIRST = pl.ds(0, STRETCH)
SECOND = pl.ds(STRETCH, STRETCH)
HALVES = (FIRST, SECOND)

O, P0, P1, P0S, P1S, R0, R1, R0S, XZ, XZS, R1S, Q0S, Q1S, Q0, Q1, OS = range(STEPS)
P, PS, R, RS, Q, QS = (P0, P1), (P0S, P1S), (R0, R1), (R0S, R1S), (Q0, Q1), (Q0S, Q1S)


def dot(a, b, ca=1, cb=0):
    return lax.dot_general(a, b, (((ca,), (cb,)), ((), ())), preferred_element_type=F32)


def kernel(order, q_in, do_in, o_in, norm_in, k_in, v_in, dq_out, dk_out, dv_out,
           qh, doh, oh, qt, dot_, nb, dl, dqa, ps, dss, kpos, qpos, kv, acc, stage,
           r_sib, r_in, comb, r_xz, comb_xz, dqb, dkb, dvb, ssem, rsem, isem, osem):
    me = lax.axis_index("ctx")
    core = lax.rem(me, 2)
    chip = me // 2
    x = lax.rem(chip, 2)
    z = chip // 2
    zp, zm, z2 = lax.rem(z + 1, 4), lax.rem(z + 3, 4), lax.rem(z + 2, 4)

    def at(zz, xx, cc):
        return (zz * 2 + xx) * 2 + cc

    sib = at(z, x, 1 - core)
    across = at(z, 1 - x, core)
    up = at(zp, x, core)
    down = at(zm, x, core)
    far = at(z2, x, core)

    def copy(n, src, dst, where):
        return pltpu.make_async_remote_copy(
            src_ref=src, dst_ref=dst, send_sem=ssem.at[n], recv_sem=rsem.at[n],
            device_id={"ctx": where}, device_id_type=pl.DeviceIdType.MESH)

    copies = {"o": (kv.at[O], kv.at[OS], sib), "xz": (kv.at[XZ], kv.at[XZS], sib),
              "x2": (comb_xz, r_xz, across), "os": (stage.at[OS], r_sib.at[0], sib),
              "xzs": (stage.at[XZS], r_sib.at[5], sib),
              "z0": (kv.at[P0, SECOND], kv.at[Q0, SECOND], up),
              "z1": (kv.at[P1, FIRST], kv.at[Q1, SECOND], down)}
    for h in range(2):
        own = kv.at[O, HALVES[h]]
        copies |= {
            f"ou{h}": (own, kv.at[P[h], SECOND], up),
            f"od{h}": (own, kv.at[P[h], FIRST], down),
            f"ox{h}": (own, kv.at[Q[h], FIRST], across),
            f"xu{h}": (kv.at[Q[h], FIRST], kv.at[R[h], SECOND], up),
            f"xd{h}": (kv.at[Q[h], FIRST], kv.at[R[h], FIRST], down),
            f"zx{h}": (kv.at[Q[h], SECOND], kv.at[XZ, HALVES[h]], across),
            f"p{h}": (kv.at[P[h]], kv.at[PS[h]], sib),
            f"q{h}": (kv.at[Q[h]], kv.at[QS[h]], sib),
            f"r{h}": (kv.at[R[h]], kv.at[RS[h]], sib),
            f"ps{h}": (stage.at[PS[h]], r_sib.at[1 + h], sib),
            f"rs{h}": (stage.at[RS[h]], r_sib.at[3 + h], sib),
            f"qs{h}": (stage.at[QS[h]], r_sib.at[6 + h], sib),
            f"pu{h}": (comb.at[h, 0], r_in.at[h, 0], up),
            f"pd{h}": (comb.at[h, 1], r_in.at[h, 1], down),
            f"ru{h}": (comb.at[2 + h, 0], r_in.at[2 + h, 0], up),
            f"rd{h}": (comb.at[2 + h, 1], r_in.at[2 + h, 1], down),
            f"qx{h}": (comb.at[4 + h, 0], r_in.at[4 + h, 0], across),
            f"qz{h}": (comb.at[4 + h, 1], r_in.at[4 + h, 1], far),
        }
    number = {name: n for n, name in enumerate(copies)}

    def start(names):
        for name in names.split():
            copy(number[name], *copies[name]).start()

    def arrived(names):
        for name in names.split():
            copy(number[name], *copies[name]).wait_recv()

    barrier = pltpu.get_barrier_semaphore()
    for other in (sib, across, up, down, far):
        pl.semaphore_signal(barrier, inc=1, device_id={"ctx": other},
                            device_id_type=pl.DeviceIdType.MESH)
    loads = [(k_in, kv.at[O, :, pl.ds(0, HD)]), (v_in, kv.at[O, :, pl.ds(HD, HD)])]
    for h in range(HEADS):
        cols, rows = pl.ds(h * HD, HD), pl.ds(h * ROWS, ROWS)
        loads += [(q_in.at[:, cols], qh.at[rows]), (do_in.at[:, cols], doh.at[rows]),
                  (o_in.at[:, cols], oh.at[rows])]
    loads = [pltpu.make_async_copy(src, dst, isem.at[n]) for n, (src, dst) in enumerate(loads)]
    for load in loads:
        load.start()
    row_iota = lax.broadcasted_iota(jnp.int32, (8, STRETCH), 1)
    col_iota = lax.broadcasted_iota(jnp.int32, (STRETCH, HD), 0)
    other_core = 1 - core
    other_x = 1 - x
    blocks = {O: (me * 2, me * 2 + 1), OS: (sib * 2, sib * 2 + 1)}
    blocks[XZ] = tuple(at(z2, other_x, core) * 2 + h for h in range(2))
    blocks[XZS] = tuple(at(z2, other_x, other_core) * 2 + h for h in range(2))
    for h in range(2):
        for block, c in ((P[h], core), (PS[h], other_core)):
            blocks[block] = (at(zp, x, c) * 2 + h, at(zm, x, c) * 2 + h)
        for block, c in ((R[h], core), (RS[h], other_core)):
            blocks[block] = (at(zp, other_x, c) * 2 + h, at(zm, other_x, c) * 2 + h)
        for block, c in ((Q[h], core), (QS[h], other_core)):
            blocks[block] = (at(z, other_x, c) * 2 + h, at(z2, x, c) * 2 + h)
    for block, stretches in blocks.items():
        for h, stretch in enumerate(stretches):
            cols = slice(h * STRETCH, (h + 1) * STRETCH)
            kpos[block, :, cols] = row_iota + order[stretch] * STRETCH
    for h in range(2):
        qpos[h * STRETCH : (h + 1) * STRETCH] = col_iota + order[me * 2 + h] * STRETCH

    dqa[...] = jnp.zeros_like(dqa)
    loads[0].wait()
    loads[1].wait()
    pl.semaphore_wait(barrier, 5)
    start("ou0 od0 ox0")

    norm = norm_in[...] * LOG2E
    norm_cols = jnp.concatenate([norm, norm], axis=0).T
    for h in range(HEADS):
        for load in loads[2 + 3 * h : 5 + 3 * h]:
            load.wait()
        if h == 2:
            start("ou1 od1 ox1 o")
        rows = slice(h * ROWS, (h + 1) * ROWS)
        do = doh[rows, :]
        qt[:, rows] = qh[rows, :].T
        dot_[:, rows] = do.T
        delta = jnp.sum(do.astype(F32) * oh[rows, :].astype(F32), axis=1, keepdims=True)
        nb[rows, :] = jnp.broadcast_to(norm_cols[:, h : h + 1], (ROWS, HD))
        dl[rows, :] = jnp.broadcast_to(delta, (ROWS, HD))

    def wide(a):
        return jnp.concatenate([a] * (KEYS // HD), axis=1)

    def compute(b):
        for h in range(HEADS):
            rows = slice(h * ROWS, (h + 1) * ROWS)
            k = kv[b, :, 0:HD]
            v = kv[b, :, HD:]
            s = dot(qh[rows, :], k, 1, 1)
            dp = dot(doh[rows, :], v, 1, 1)
            seen = kpos[b, 0:1, :] <= wide(qpos[...])
            p = jnp.exp2(jnp.where(seen, s * (SCALE * LOG2E) - wide(nb[rows, :]), HIDDEN))
            ds = (p * (dp - wide(dl[rows, :]))).astype(BF16)
            ps[rows, :] = p.astype(BF16)
            dss[rows, :] = ds
            dqa[rows, :] += dot(ds, k)
        dk = dot(qt[...], dss[...])
        dv = dot(dot_[...], ps[...])
        acc[b, 0:HD] = dk
        acc[b, HD:] = dv
        stage[b, 0:HD] = dk.astype(BF16)
        stage[b, HD:] = dv.astype(BF16)

    def combine(n, block, sib_part):
        total = acc[block] + r_sib[sib_part].astype(F32)
        for part in range(2):
            cols = slice(part * STRETCH, (part + 1) * STRETCH)
            comb[n, part] = total[:, cols].astype(BF16)

    def combine_q(h):
        cols = slice(h * STRETCH, (h + 1) * STRETCH)
        total = acc[Q[h]] + r_sib[6 + h].astype(F32)
        comb[4 + h, 0] = (total[:, :STRETCH] + r_in[2 + h, 0].astype(F32)
                          + r_in[2 + h, 1].astype(F32)).astype(BF16)
        comb[4 + h, 1] = (total[:, STRETCH:] + r_xz[:, cols].astype(F32)).astype(BF16)

    def before(t):
        if t == P0:
            arrived("ou0 od0")
            start("z0 p0")
            arrived("ox0")
            start("xd0")
        if t == P1:
            arrived("ou1 od1")
            start("z1 xu0 p1")
        if t == P0S:
            arrived("ox1")
            start("xu1 xd1")
            arrived("p0")
        if t == P1S:
            start("ps0")
            arrived("p1 z0 z1")
            start("zx0 zx1 q0 q1")
        if t == R0:
            start("ps1")
            arrived("xu0 xd0")
            start("r0")
            arrived("ps0")
            combine(0, P0, 1)
            start("pu0 pd0")
        if t == R1:
            arrived("xu1 xd1")
            start("r1")
            arrived("ps1")
            combine(1, P1, 2)
            start("pu1 pd1")
        if t == R0S:
            arrived("r0")
        if t == XZ:
            start("rs0")
            arrived("zx0 zx1")
            start("xz")
        if t == XZS:
            arrived("xz rs0")
            combine(2, R0, 3)
            start("ru0 rd0")
        if t == R1S:
            start("xzs")
            arrived("r1")
        if t == Q0S:
            start("rs1")
            arrived("xzs")
            comb_xz[...] = (acc[XZ] + r_sib[5].astype(F32)).astype(BF16)
            start("x2")
            arrived("q0")
        if t == Q1S:
            start("qs0")
            arrived("rs1")
            combine(3, R1, 4)
            start("ru1 rd1")
            arrived("q1")
        if t == Q0:
            start("qs1")
        if t == Q1:
            arrived("qs0 ru0 rd0 x2")
            combine_q(0)
            start("qx0 qz0")
        if t == OS:
            arrived("qs1 ru1 rd1")
            combine_q(1)
            start("qx1 qz1")
            arrived("o")

    def body(t, _):
        for n in range(1, STEPS):
            pl.when(t == n)(lambda n=n: before(n))
        compute(t)
        return 0

    lax.fori_loop(0, STEPS, body, 0)
    start("os")
    outs = []
    for h in range(HEADS):
        cols = slice(h * HD, (h + 1) * HD)
        dqb[:, cols] = (dqa[h * ROWS : (h + 1) * ROWS, :] * SCALE).astype(BF16)
    outs.append(pltpu.make_async_copy(dqb, dq_out, osem.at[0]))
    outs[0].start()
    arrived("os")
    arrived("pu0 pd0 pu1 pd1")
    for h in range(2):
        cols = slice(h * STRETCH, (h + 1) * STRETCH)
        acc[O, :, cols] += (r_sib[0, :, cols].astype(F32) + r_in[h, 0].astype(F32)
                            + r_in[h, 1].astype(F32))
    for h in range(2):
        cols = slice(h * STRETCH, (h + 1) * STRETCH)
        arrived(f"qx{h} qz{h}")
        total = acc[O, :, cols] + r_in[4 + h, 0].astype(F32) + r_in[4 + h, 1].astype(F32)
        dkb[cols, :] = (total[0:HD] * SCALE).astype(BF16).T
        dvb[cols, :] = total[HD:].astype(BF16).T
        for n, (src, dst) in enumerate(((dkb, dk_out), (dvb, dv_out))):
            out = pltpu.make_async_copy(src.at[HALVES[h]], dst.at[HALVES[h]],
                                        osem.at[1 + 2 * h + n])
            out.start()
            outs.append(out)
    for name in copies:
        copy(number[name], *copies[name]).wait_send()
    for out in outs:
        out.wait()


def hand_over(dq, dk, dv, dq_out, dk_out, dv_out, dqb, dkb, dvb, sem_in, sem_out):
    moves = []
    for n, refs in enumerate(((dq, dqb, dq_out), (dk, dkb, dk_out), (dv, dvb, dv_out))):
        for h in range(2):
            src, mid, dst = (ref.at[HALVES[h]] for ref in refs)
            moves.append((pltpu.make_async_copy(src, mid, sem_in.at[2 * n + h]),
                          pltpu.make_async_copy(mid, dst, sem_out.at[2 * n + h])))
    for load, _ in moves:
        load.start()
    for load, store in moves:
        load.wait()
        store.start()
    for _, store in moves:
        store.wait()


def shards(queries, keys, values, outputs, out_grads, log_norms, stretch_order):
    rows = HEADS * ROWS
    anywhere = pl.BlockSpec(memory_space=pl.ANY)
    shapes = [
        jax.ShapeDtypeStruct((ROWS, HEADS * HD), BF16),
        jax.ShapeDtypeStruct((ROWS, HD), BF16),
        jax.ShapeDtypeStruct((ROWS, HD), BF16),
    ]
    grads = pl.pallas_call(
        kernel,
        out_shape=shapes,
        in_specs=[pl.BlockSpec(memory_space=pltpu.SMEM), anywhere, anywhere, anywhere,
                  pl.BlockSpec(memory_space=pltpu.VMEM), anywhere, anywhere],
        out_specs=[anywhere] * 3,
        scratch_shapes=[
            pltpu.VMEM((rows, HD), BF16),
            pltpu.VMEM((rows, HD), BF16),
            pltpu.VMEM((rows, HD), BF16),
            pltpu.VMEM((HD, rows), BF16),
            pltpu.VMEM((HD, rows), BF16),
            pltpu.VMEM((rows, HD), F32),
            pltpu.VMEM((rows, HD), F32),
            pltpu.VMEM((rows, HD), F32),
            pltpu.VMEM((rows, KEYS), BF16),
            pltpu.VMEM((rows, KEYS), BF16),
            pltpu.VMEM((STEPS, 8, KEYS), jnp.int32),
            pltpu.VMEM((ROWS, HD), jnp.int32),
            pltpu.VMEM((STEPS, KEYS, 2 * HD), BF16),
            pltpu.VMEM((STEPS, 2 * HD, KEYS), F32),
            pltpu.VMEM((STEPS, 2 * HD, KEYS), BF16),
            pltpu.VMEM((8, 2 * HD, KEYS), BF16),
            pltpu.VMEM((6, 2, 2 * HD, STRETCH), BF16),
            pltpu.VMEM((6, 2, 2 * HD, STRETCH), BF16),
            pltpu.VMEM((2 * HD, KEYS), BF16),
            pltpu.VMEM((2 * HD, KEYS), BF16),
            pltpu.VMEM((ROWS, HEADS * HD), BF16),
            pltpu.VMEM((ROWS, HD), BF16),
            pltpu.VMEM((ROWS, HD), BF16),
            pltpu.SemaphoreType.DMA((43,)),
            pltpu.SemaphoreType.DMA((43,)),
            pltpu.SemaphoreType.DMA((14,)),
            pltpu.SemaphoreType.DMA((5,)),
        ],
        compiler_params=pltpu.CompilerParams(
            vmem_limit_bytes=58 * 2**20, collective_id=0, has_side_effects=True
        ),
    )(stretch_order, queries, out_grads, outputs, log_norms, keys, values)
    return pl.pallas_call(
        hand_over,
        out_shape=shapes,
        in_specs=[anywhere] * 3,
        out_specs=[anywhere] * 3,
        scratch_shapes=[pltpu.VMEM(shape.shape, BF16) for shape in shapes]
        + [pltpu.SemaphoreType.DMA((6,)), pltpu.SemaphoreType.DMA((6,))],
    )(*grads)


def solution(mesh):
    return jax.shard_map(
        shards,
        mesh=mesh,
        in_specs=(
            PartitionSpec(("dp", "ctx"), "tp"),
            PartitionSpec(("dp", "ctx"), "tp"),
            PartitionSpec(("dp", "ctx"), "tp"),
            PartitionSpec(("dp", "ctx"), "tp"),
            PartitionSpec(("dp", "ctx"), "tp"),
            PartitionSpec("tp", ("dp", "ctx")),
            PartitionSpec("dp"),
        ),
        out_specs=(PartitionSpec(("dp", "ctx"), "tp"), PartitionSpec(("dp", "ctx"), "tp"), PartitionSpec(("dp", "ctx"), "tp")),
        check_vma=False,
    )
```

```python
import jax
import jax.numpy as jnp
from jax import lax
from jax.experimental import pallas as pl
from jax.experimental.pallas import tpu as pltpu
from jax.sharding import PartitionSpec

HD = 128
HEADS = 4
STRETCH = 256
ROWS = 512
KEYS = 512
STEPS = 16
F32 = jnp.float32
BF16 = jnp.bfloat16
LOG2E = 1.4426950408889634
SCALE = HD ** (-0.5)
HIDDEN = -1e30
FIRST = pl.ds(0, STRETCH)
SECOND = pl.ds(STRETCH, STRETCH)
HALVES = (FIRST, SECOND)

O, P0, P1, P0S, P1S, R0, R1, R0S, XZ, XZS, R1S, Q0S, Q1S, Q0, Q1, OS = range(STEPS)
P, PS, R, RS, Q, QS = (P0, P1), (P0S, P1S), (R0, R1), (R0S, R1S), (Q0, Q1), (Q0S, Q1S)


def dot(a, b, ca=1, cb=0):
    return lax.dot_general(a, b, (((ca,), (cb,)), ((), ())), preferred_element_type=F32)


def kernel(order, q_in, do_in, o_in, norm_in, k_in, v_in, dq_out, dk_out, dv_out,
           qh, doh, oh, qt, dot_, nb, dl, dqa, ps, dss, kpos, qpos, kv, acc, stage,
           r_sib, r_in, comb, r_xz, comb_xz, dqb, dkb, dvb, ssem, rsem, isem, osem):
    me = lax.axis_index("ctx")
    core = lax.rem(me, 2)
    chip = me // 2
    x = lax.rem(chip, 2)
    z = chip // 2
    zp, zm, z2 = lax.rem(z + 1, 4), lax.rem(z + 3, 4), lax.rem(z + 2, 4)

    def at(zz, xx, cc):
        return (zz * 2 + xx) * 2 + cc

    sib = at(z, x, 1 - core)
    across = at(z, 1 - x, core)
    up = at(zp, x, core)
    down = at(zm, x, core)
    far = at(z2, x, core)

    def copy(n, src, dst, where):
        return pltpu.make_async_remote_copy(
            src_ref=src, dst_ref=dst, send_sem=ssem.at[n], recv_sem=rsem.at[n],
            device_id={"ctx": where}, device_id_type=pl.DeviceIdType.MESH)

    copies = {"o": (kv.at[O], kv.at[OS], sib), "xz": (kv.at[XZ], kv.at[XZS], sib),
              "x2": (comb_xz, r_xz, across), "os": (stage.at[OS], r_sib.at[0], sib),
              "xzs": (stage.at[XZS], r_sib.at[5], sib),
              "z0": (kv.at[P0, SECOND], kv.at[Q0, SECOND], up),
              "z1": (kv.at[P1, FIRST], kv.at[Q1, SECOND], down)}
    for h in range(2):
        own = kv.at[O, HALVES[h]]
        copies |= {
            f"ou{h}": (own, kv.at[P[h], SECOND], up),
            f"od{h}": (own, kv.at[P[h], FIRST], down),
            f"ox{h}": (own, kv.at[Q[h], FIRST], across),
            f"xu{h}": (kv.at[Q[h], FIRST], kv.at[R[h], SECOND], up),
            f"xd{h}": (kv.at[Q[h], FIRST], kv.at[R[h], FIRST], down),
            f"zx{h}": (kv.at[Q[h], SECOND], kv.at[XZ, HALVES[h]], across),
            f"p{h}": (kv.at[P[h]], kv.at[PS[h]], sib),
            f"q{h}": (kv.at[Q[h]], kv.at[QS[h]], sib),
            f"r{h}": (kv.at[R[h]], kv.at[RS[h]], sib),
            f"ps{h}": (stage.at[PS[h]], r_sib.at[1 + h], sib),
            f"rs{h}": (stage.at[RS[h]], r_sib.at[3 + h], sib),
            f"qs{h}": (stage.at[QS[h]], r_sib.at[6 + h], sib),
            f"pu{h}": (comb.at[h, 0], r_in.at[h, 0], up),
            f"pd{h}": (comb.at[h, 1], r_in.at[h, 1], down),
            f"ru{h}": (comb.at[2 + h, 0], r_in.at[2 + h, 0], up),
            f"rd{h}": (comb.at[2 + h, 1], r_in.at[2 + h, 1], down),
            f"qx{h}": (comb.at[4 + h, 0], r_in.at[4 + h, 0], across),
            f"qz{h}": (comb.at[4 + h, 1], r_in.at[4 + h, 1], far),
        }
    number = {name: n for n, name in enumerate(copies)}

    def start(names):
        for name in names.split():
            copy(number[name], *copies[name]).start()

    def arrived(names):
        for name in names.split():
            copy(number[name], *copies[name]).wait_recv()

    barrier = pltpu.get_barrier_semaphore()
    for other in (sib, across, up, down, far):
        pl.semaphore_signal(barrier, inc=1, device_id={"ctx": other},
                            device_id_type=pl.DeviceIdType.MESH)
    loads = [(k_in, kv.at[O, :, pl.ds(0, HD)]), (v_in, kv.at[O, :, pl.ds(HD, HD)])]
    for h in range(HEADS):
        cols, rows = pl.ds(h * HD, HD), pl.ds(h * ROWS, ROWS)
        loads += [(q_in.at[:, cols], qh.at[rows]), (do_in.at[:, cols], doh.at[rows]),
                  (o_in.at[:, cols], oh.at[rows])]
    loads = [pltpu.make_async_copy(src, dst, isem.at[n]) for n, (src, dst) in enumerate(loads)]
    for load in loads:
        load.start()
    row_iota = lax.broadcasted_iota(jnp.int32, (8, STRETCH), 1)
    col_iota = lax.broadcasted_iota(jnp.int32, (STRETCH, HD), 0)
    other_core = 1 - core
    other_x = 1 - x
    blocks = {O: (me * 2, me * 2 + 1), OS: (sib * 2, sib * 2 + 1)}
    blocks[XZ] = tuple(at(z2, other_x, core) * 2 + h for h in range(2))
    blocks[XZS] = tuple(at(z2, other_x, other_core) * 2 + h for h in range(2))
    for h in range(2):
        for block, c in ((P[h], core), (PS[h], other_core)):
            blocks[block] = (at(zp, x, c) * 2 + h, at(zm, x, c) * 2 + h)
        for block, c in ((R[h], core), (RS[h], other_core)):
            blocks[block] = (at(zp, other_x, c) * 2 + h, at(zm, other_x, c) * 2 + h)
        for block, c in ((Q[h], core), (QS[h], other_core)):
            blocks[block] = (at(z, other_x, c) * 2 + h, at(z2, x, c) * 2 + h)
    for block, stretches in blocks.items():
        for h, stretch in enumerate(stretches):
            cols = slice(h * STRETCH, (h + 1) * STRETCH)
            kpos[block, :, cols] = row_iota + order[stretch] * STRETCH
    for h in range(2):
        qpos[h * STRETCH : (h + 1) * STRETCH] = col_iota + order[me * 2 + h] * STRETCH

    dqa[...] = jnp.zeros_like(dqa)
    loads[0].wait()
    loads[1].wait()
    pl.semaphore_wait(barrier, 5)
    start("ou0 od0 ox0")

    norm = norm_in[...] * LOG2E
    norm_cols = jnp.concatenate([norm, norm], axis=0).T
    for h in range(HEADS):
        for load in loads[2 + 3 * h : 5 + 3 * h]:
            load.wait()
        if h == 2:
            start("ou1 od1 ox1 o")
        rows = slice(h * ROWS, (h + 1) * ROWS)
        do = doh[rows, :]
        qt[:, rows] = qh[rows, :].T
        dot_[:, rows] = do.T
        delta = jnp.sum(do.astype(F32) * oh[rows, :].astype(F32), axis=1, keepdims=True)
        nb[rows, :] = jnp.broadcast_to(norm_cols[:, h : h + 1], (ROWS, HD))
        dl[rows, :] = jnp.broadcast_to(delta, (ROWS, HD))

    def wide(a):
        return jnp.concatenate([a] * (KEYS // HD), axis=1)

    def compute(b):
        for h in range(HEADS):
            rows = slice(h * ROWS, (h + 1) * ROWS)
            k = kv[b, :, 0:HD]
            v = kv[b, :, HD:]
            s = dot(qh[rows, :], k, 1, 1)
            dp = dot(doh[rows, :], v, 1, 1)
            seen = kpos[b, 0:1, :] <= wide(qpos[...])
            p = jnp.exp2(jnp.where(seen, s * (SCALE * LOG2E) - wide(nb[rows, :]), HIDDEN))
            ds = (p * (dp - wide(dl[rows, :]))).astype(BF16)
            ps[rows, :] = p.astype(BF16)
            dss[rows, :] = ds
            dqa[rows, :] += dot(ds, k)
        dk = dot(qt[...], dss[...])
        dv = dot(dot_[...], ps[...])
        acc[b, 0:HD] = dk
        acc[b, HD:] = dv
        stage[b, 0:HD] = dk.astype(BF16)
        stage[b, HD:] = dv.astype(BF16)

    def combine(n, block, sib_part):
        total = acc[block] + r_sib[sib_part].astype(F32)
        for part in range(2):
            cols = slice(part * STRETCH, (part + 1) * STRETCH)
            comb[n, part] = total[:, cols].astype(BF16)

    def combine_q(h):
        cols = slice(h * STRETCH, (h + 1) * STRETCH)
        total = acc[Q[h]] + r_sib[6 + h].astype(F32)
        comb[4 + h, 0] = (total[:, :STRETCH] + r_in[2 + h, 0].astype(F32)
                          + r_in[2 + h, 1].astype(F32)).astype(BF16)
        comb[4 + h, 1] = (total[:, STRETCH:] + r_xz[:, cols].astype(F32)).astype(BF16)

    def before(t):
        if t == P0:
            arrived("ou0 od0")
            start("z0 p0")
            arrived("ox0")
            start("xd0 xu0")
        if t == P1:
            arrived("ou1 od1")
            start("z1 p1")
        if t == P0S:
            arrived("ox1")
            start("xu1 xd1")
            arrived("p0")
        if t == P1S:
            start("ps0")
            arrived("p1 z0 z1")
            start("zx0 zx1 q0 q1")
        if t == R0:
            start("ps1")
            arrived("xu0 xd0")
            start("r0")
            arrived("ps0")
            combine(0, P0, 1)
            start("pu0 pd0")
        if t == R1:
            arrived("xu1 xd1")
            start("r1")
            arrived("ps1")
            combine(1, P1, 2)
            start("pu1 pd1")
        if t == R0S:
            arrived("r0")
        if t == XZ:
            start("rs0")
            arrived("zx0 zx1")
            start("xz")
        if t == XZS:
            arrived("xz rs0")
            combine(2, R0, 3)
            start("ru0 rd0")
        if t == R1S:
            start("xzs")
            arrived("r1")
        if t == Q0S:
            start("rs1")
            arrived("xzs")
            comb_xz[...] = (acc[XZ] + r_sib[5].astype(F32)).astype(BF16)
            start("x2")
            arrived("q0")
        if t == Q1S:
            start("qs0")
            arrived("rs1")
            combine(3, R1, 4)
            start("ru1 rd1")
            arrived("q1")
        if t == Q0:
            start("qs1")
        if t == Q1:
            arrived("qs0 ru0 rd0 x2")
            combine_q(0)
            start("qx0 qz0")
        if t == OS:
            arrived("qs1 ru1 rd1")
            combine_q(1)
            start("qx1 qz1")
            arrived("o")

    def body(t, _):
        for n in range(1, STEPS):
            pl.when(t == n)(lambda n=n: before(n))
        compute(t)
        return 0

    lax.fori_loop(0, STEPS, body, 0)
    start("os")
    outs = []
    for h in range(HEADS):
        cols = slice(h * HD, (h + 1) * HD)
        dqb[:, cols] = (dqa[h * ROWS : (h + 1) * ROWS, :] * SCALE).astype(BF16)
    outs.append(pltpu.make_async_copy(dqb, dq_out, osem.at[0]))
    outs[0].start()
    arrived("os")
    arrived("pu0 pd0 pu1 pd1")
    for h in range(2):
        cols = slice(h * STRETCH, (h + 1) * STRETCH)
        acc[O, :, cols] += (r_sib[0, :, cols].astype(F32) + r_in[h, 0].astype(F32)
                            + r_in[h, 1].astype(F32))
    for h in range(2):
        cols = slice(h * STRETCH, (h + 1) * STRETCH)
        arrived(f"qx{h} qz{h}")
        total = acc[O, :, cols] + r_in[4 + h, 0].astype(F32) + r_in[4 + h, 1].astype(F32)
        dkb[cols, :] = (total[0:HD] * SCALE).astype(BF16).T
        dvb[cols, :] = total[HD:].astype(BF16).T
        for n, (src, dst) in enumerate(((dkb, dk_out), (dvb, dv_out))):
            out = pltpu.make_async_copy(src.at[HALVES[h]], dst.at[HALVES[h]],
                                        osem.at[1 + 2 * h + n])
            out.start()
            outs.append(out)
    for name in copies:
        copy(number[name], *copies[name]).wait_send()
    for out in outs:
        out.wait()


def hand_over(dq, dk, dv, dq_out, dk_out, dv_out, dqb, dkb, dvb, sem_in, sem_out):
    moves = []
    for n, refs in enumerate(((dq, dqb, dq_out), (dk, dkb, dk_out), (dv, dvb, dv_out))):
        for h in range(2):
            src, mid, dst = (ref.at[HALVES[h]] for ref in refs)
            moves.append((pltpu.make_async_copy(src, mid, sem_in.at[2 * n + h]),
                          pltpu.make_async_copy(mid, dst, sem_out.at[2 * n + h])))
    for load, _ in moves:
        load.start()
    for load, store in moves:
        load.wait()
        store.start()
    for _, store in moves:
        store.wait()


def shards(queries, keys, values, outputs, out_grads, log_norms, stretch_order):
    rows = HEADS * ROWS
    anywhere = pl.BlockSpec(memory_space=pl.ANY)
    shapes = [
        jax.ShapeDtypeStruct((ROWS, HEADS * HD), BF16),
        jax.ShapeDtypeStruct((ROWS, HD), BF16),
        jax.ShapeDtypeStruct((ROWS, HD), BF16),
    ]
    grads = pl.pallas_call(
        kernel,
        out_shape=shapes,
        in_specs=[pl.BlockSpec(memory_space=pltpu.SMEM), anywhere, anywhere, anywhere,
                  pl.BlockSpec(memory_space=pltpu.VMEM), anywhere, anywhere],
        out_specs=[anywhere] * 3,
        scratch_shapes=[
            pltpu.VMEM((rows, HD), BF16),
            pltpu.VMEM((rows, HD), BF16),
            pltpu.VMEM((rows, HD), BF16),
            pltpu.VMEM((HD, rows), BF16),
            pltpu.VMEM((HD, rows), BF16),
            pltpu.VMEM((rows, HD), F32),
            pltpu.VMEM((rows, HD), F32),
            pltpu.VMEM((rows, HD), F32),
            pltpu.VMEM((rows, KEYS), BF16),
            pltpu.VMEM((rows, KEYS), BF16),
            pltpu.VMEM((STEPS, 8, KEYS), jnp.int32),
            pltpu.VMEM((ROWS, HD), jnp.int32),
            pltpu.VMEM((STEPS, KEYS, 2 * HD), BF16),
            pltpu.VMEM((STEPS, 2 * HD, KEYS), F32),
            pltpu.VMEM((STEPS, 2 * HD, KEYS), BF16),
            pltpu.VMEM((8, 2 * HD, KEYS), BF16),
            pltpu.VMEM((6, 2, 2 * HD, STRETCH), BF16),
            pltpu.VMEM((6, 2, 2 * HD, STRETCH), BF16),
            pltpu.VMEM((2 * HD, KEYS), BF16),
            pltpu.VMEM((2 * HD, KEYS), BF16),
            pltpu.VMEM((ROWS, HEADS * HD), BF16),
            pltpu.VMEM((ROWS, HD), BF16),
            pltpu.VMEM((ROWS, HD), BF16),
            pltpu.SemaphoreType.DMA((43,)),
            pltpu.SemaphoreType.DMA((43,)),
            pltpu.SemaphoreType.DMA((14,)),
            pltpu.SemaphoreType.DMA((5,)),
        ],
        compiler_params=pltpu.CompilerParams(
            vmem_limit_bytes=58 * 2**20, collective_id=0, has_side_effects=True
        ),
    )(stretch_order, queries, out_grads, outputs, log_norms, keys, values)
    return pl.pallas_call(
        hand_over,
        out_shape=shapes,
        in_specs=[anywhere] * 3,
        out_specs=[anywhere] * 3,
        scratch_shapes=[pltpu.VMEM(shape.shape, BF16) for shape in shapes]
        + [pltpu.SemaphoreType.DMA((6,)), pltpu.SemaphoreType.DMA((6,))],
    )(*grads)


def solution(mesh):
    return jax.shard_map(
        shards,
        mesh=mesh,
        in_specs=(
            PartitionSpec(("dp", "ctx"), "tp"),
            PartitionSpec(("dp", "ctx"), "tp"),
            PartitionSpec(("dp", "ctx"), "tp"),
            PartitionSpec(("dp", "ctx"), "tp"),
            PartitionSpec(("dp", "ctx"), "tp"),
            PartitionSpec("tp", ("dp", "ctx")),
            PartitionSpec("dp"),
        ),
        out_specs=(PartitionSpec(("dp", "ctx"), "tp"), PartitionSpec(("dp", "ctx"), "tp"), PartitionSpec(("dp", "ctx"), "tp")),
        check_vma=False,
    )
```
